32 devices in a mesh: groups: 2 (over y), ctx: 4 (over z), tp: 4 (over x, core).
Axes of the slice: x: 2, y: 2, z: 4, core: 2. Of those that a mesh axis runs over, the one named last changes fastest.
Arguments:
- queries: bfloat16 [2048, 4096], P(('groups', 'ctx'), 'tp'), parts along dimension 0, may hold values from -24 to 24
- response_keys: bfloat16 [2048, 512], P(('groups', 'ctx'), 'tp'), parts along dimension 0, may hold values from -4.5 to 4.5
- response_values: bfloat16 [2048, 512], P(('groups', 'ctx'), 'tp'), parts along dimension 0, may hold values from -6 to 6
- prompt_keys: bfloat16 [2048, 512], P(('groups', 'ctx'), 'tp'), parts along dimension 0, may hold values from -4.5 to 4.5
- prompt_values: bfloat16 [2048, 512], P(('groups', 'ctx'), 'tp'), parts along dimension 0, may hold values from -6 to 6
- response_lengths: int32 [12], P('groups'), parts along dimension 0, may hold values from 1 to 256, 1024 in all
- out_weight: bfloat16 [4096, 4096], P('tp'), may hold values from -0.75 to 0.75
Outputs:
- projected: bfloat16 [2048, 4096], P(('groups', 'ctx'), 'tp'), parts along dimension 0
The draws below stay inside these ranges and needn't reach their ends.
There are 2 independent parts, one for each index of `groups`. The reference program is written for one: setup_inputs(seed, part) draws one part's arguments, and reference() takes and returns one part's arrays. A program takes and returns all parts, laid end to end along the dimension named above; an argument that names none is the same for every part. Nothing has to cross between parts.
Inputs may be any that keep to these rules, and one draw needn't show every extreme that they name: `response_lengths`: they sum to 1024; the longest is exactly 256.
All inputs are finite; a program needn't handle non-finite values.
Results may differ from the reference program's by a relative error of at most 0.013.
Values may be sent and summed in bfloat16 or wider, within the bound.
A program may use at most 64 MiB of HBM per device.

```python
import math
import jax
import jax.numpy as jnp
import numpy as np
from jax import lax

HD = 128
HEADS = 32
KVH = 4
DOUT = 4096
LEN_MAX = 256
TOKENS = 1024
PROMPT = 1024
RESPONSES = 6
N_TP = 4


def shared_keys(key):
    first_key = jax.random.fold_in(key, 0)
    shape = (PROMPT, KVH * HD)
    normal_part = jnp.clip(jax.random.normal(first_key, shape, jnp.float32) * 1.4, -4.5, 4.5)
    base = normal_part
    evens = base[0::2]
    odds = base[1::2]
    return jnp.stack([evens, odds], axis=1).reshape(PROMPT, KVH * HD)


def draw_prompt_keys(key, part):
    keys = shared_keys(key)
    return keys.astype(jnp.bfloat16)


def draw_queries(key, part):
    shape = (TOKENS, HEADS * HD)
    key = jax.random.fold_in(key, 5)
    values = jnp.clip(jax.random.normal(key, shape, jnp.float32) * 1.4, -4.5, 4.5)
    return values.astype(jnp.bfloat16)


def block_levels(key, shape, pieces, least, largest):
    def one(axis_at, shards_of):
        steps = jax.random.uniform(jax.random.fold_in(jax.random.fold_in(key, 6), axis_at), (shards_of,), jnp.float32, least / len(pieces), largest / len(pieces))
        return jnp.repeat(jnp.exp(steps), shape[axis_at] // shards_of).reshape((-1,) + (1,) * (len(shape) - axis_at - 1))

    factor_of = one(*pieces[0])
    for cut in pieces[1:]:
        factor_of = factor_of * one(*cut)
    return factor_of


def profile(count, total, limit, lean):
    weights = [(1 << 20) // math.isqrt(grade ** lean) + 1 for grade in range(2, count + 1)]
    rest, given = total - limit - (count - 1), [1] * (count - 1)
    while rest > 0:
        candidates = [i for i in range(count - 1) if given[i] < limit]
        pool, remaining = sum([weights[i] for i in candidates]), rest
        for i in candidates:
            extra = min(limit - given[i], max(1, remaining * weights[i] // pool), rest)
            given[i] = given[i] + extra
            rest = rest - extra
    return np.array([limit] + given)


def ragged(own_key, amount, total, reach, skew):
    if amount == 2:
        one = jax.random.randint(own_key, (), max(1, total - reach), min(reach, total - 1) + 1)
        return jnp.stack([one, total - one])
    tallies = jnp.asarray(profile(amount, total, reach, skew), jnp.int32)
    couples = (amount - 1) // 2
    source_of, receiver = tallies[1:1 + 2 * couples:2], tallies[2:2 + 2 * couples:2]
    slack = jnp.minimum(source_of - 1, reach - receiver)
    passed = jax.random.randint(jax.random.fold_in(own_key, 1), (couples,), 0, 1 << 20) % (slack + 1)
    tallies = tallies.at[1:1 + 2 * couples:2].set(source_of - passed).at[2:2 + 2 * couples:2].set(receiver + passed)
    return tallies[jax.random.permutation(jax.random.fold_in(own_key, 2), amount)]


def gaussian(rng, shape, scale, bound, shards=(), kind=jnp.bfloat16):
    result = scale * jax.random.normal(rng, shape, jnp.float32)
    if shards:
        result = result * block_levels(rng, shape, shards, -0.22, 0.18)
    return jnp.clip(result, -bound, bound).astype(kind)


def setup_inputs(seed: int = 0, part: int = 0) -> dict:
    key_of = jax.random.split(jax.random.key(seed), 8)
    part_keys = jax.random.split(jax.random.fold_in(key_of[7], part), 8)
    queries = draw_queries(jax.random.fold_in(jax.random.fold_in(key_of[7], part), 71), part)
    response_keys = gaussian(part_keys[1], (TOKENS, KVH * HD), 1.4, 4.5, ((0, 4), (1, 4)))
    response_values = gaussian(part_keys[2], (TOKENS, KVH * HD), 1.0, 6.0, ((0, 4), (1, 4)))
    prompt_keys = draw_prompt_keys(jax.random.fold_in(jax.random.fold_in(key_of[7], part), 71), part)
    prompt_values = gaussian(part_keys[4], (PROMPT, KVH * HD), 1.0, 6.0, ((0, 4), (1, 4)))
    response_lengths = ragged(part_keys[5], RESPONSES, TOKENS, LEN_MAX, 1).astype(jnp.int32)
    out_weight = gaussian(key_of[6], (HEADS * HD, DOUT), (HEADS * HD // 64) ** -0.5, 0.75, ((0, 4),))
    return {"queries": queries, "response_keys": response_keys, "response_values": response_values, "prompt_keys": prompt_keys, "prompt_values": prompt_values, "response_lengths": response_lengths, "out_weight": out_weight}


def attend_head(query_head, prompt_k, prompt_v, window_k, window_v, allowed):
    scale = 1.0 / (HD ** 0.5)
    prompt_scores = jnp.einsum('rgd,sd->grs', query_head, prompt_k) * scale
    window_scores = jnp.einsum('rgd,sd->grs', query_head, window_k) * scale
    window_scores = jnp.where(allowed[None, :, :], window_scores, -jnp.inf)
    scores = jnp.concatenate([prompt_scores, window_scores], axis=-1)
    top = jnp.max(scores, axis=-1, keepdims=True)
    weights = jnp.exp(scores - top)
    total = jnp.sum(weights, axis=-1)
    rounded = lax.optimization_barrier(weights.astype(jnp.bfloat16)).astype(jnp.float32)
    values = jnp.concatenate([prompt_v, window_v], axis=0)
    summed = jnp.einsum('grs,sd->grd', rounded, values)
    return summed / total[:, :, None]


def reference(queries, response_keys, response_values, prompt_keys, prompt_values, response_lengths, out_weight):
    group = HEADS // KVH
    kv_cols = KVH * HD
    block = min(TOKENS, 512)
    blocks = TOKENS // block
    lengths = response_lengths.astype(jnp.int32)
    starts = (jnp.cumsum(lengths) - lengths).astype(jnp.int32)
    positions = jnp.arange(TOKENS, dtype=jnp.int32)
    first = jnp.max(jnp.where(starts[None, :] <= positions[:, None], starts[None, :], 0), axis=1).astype(jnp.int32)
    padded_k = jnp.concatenate([jnp.zeros((LEN_MAX, kv_cols), response_keys.dtype), response_keys], axis=0)
    padded_v = jnp.concatenate([jnp.zeros((LEN_MAX, kv_cols), response_values.dtype), response_values], axis=0)
    prompt_k = prompt_keys.astype(jnp.float32).reshape(PROMPT, KVH, HD)
    prompt_v = prompt_values.astype(jnp.float32).reshape(PROMPT, KVH, HD)

    def per_block(index):
        begin = (index * block).astype(jnp.int32)
        query_rows = lax.dynamic_slice_in_dim(queries, begin, block, 0).astype(jnp.float32)
        query_rows = query_rows.reshape(block, KVH, group, HD)
        window_k = lax.dynamic_slice_in_dim(padded_k, begin, LEN_MAX + block, 0).astype(jnp.float32)
        window_v = lax.dynamic_slice_in_dim(padded_v, begin, LEN_MAX + block, 0).astype(jnp.float32)
        window_k = window_k.reshape(LEN_MAX + block, KVH, HD)
        window_v = window_v.reshape(LEN_MAX + block, KVH, HD)
        key_pos = begin - LEN_MAX + jnp.arange(LEN_MAX + block, dtype=jnp.int32)
        query_pos = lax.dynamic_slice_in_dim(positions, begin, block, 0)
        query_first = lax.dynamic_slice_in_dim(first, begin, block, 0)
        allowed = (key_pos[None, :] >= query_first[:, None]) & (key_pos[None, :] <= query_pos[:, None])
        outputs = []
        for head in range(KVH):
            outputs.append(attend_head(query_rows[:, head], prompt_k[:, head], prompt_v[:, head], window_k[:, head], window_v[:, head], allowed))
        stacked = jnp.stack(outputs, axis=0)
        return jnp.transpose(stacked, (2, 0, 1, 3)).reshape(block, HEADS * HD)

    attended = lax.map(per_block, jnp.arange(blocks, dtype=jnp.int32))
    attended = attended.reshape(TOKENS, HEADS * HD).astype(jnp.bfloat16)
    width = HEADS * HD // N_TP
    summed = jnp.zeros((TOKENS, DOUT), jnp.float32)
    for part in range(N_TP):
        partial_value = jnp.dot(attended[:, part * width:(part + 1) * width], out_weight[part * width:(part + 1) * width], preferred_element_type=jnp.float32)
        summed = summed + lax.optimization_barrier(partial_value.astype(jnp.bfloat16)).astype(jnp.float32)
    return summed.astype(jnp.bfloat16)
```

```python
import functools

import jax
import jax.numpy as jnp
from jax import lax
from jax.experimental import pallas as pl
from jax.experimental.pallas import tpu as pltpu
from jax.sharding import PartitionSpec as P

HD = 128
SUB = 256
MESH = pl.DeviceIdType.MESH
SCALE = 1.4426950408889634 / HD**0.5
MASKED = -1e30


def kernel(
    n,
    n_tp,
    q_hbm,
    rk_hbm,
    rv_hbm,
    pk_hbm,
    pv_hbm,
    lengths,
    w_hbm,
    out_hbm,
    q,
    w,
    key_all,
    value_all,
    resp_k,
    resp_v,
    bias,
    acc,
    tops,
    att,
    send1,
    recv1,
    send2,
    recv2,
    near,
    out,
    in_sem,
    w_sem,
    out_sem,
    gather_send,
    gather_recv,
    resp_send,
    resp_recv,
    send1_sem,
    recv1_sem,
    send2_sem,
    recv2_sem,
):
    me = lax.axis_index("ctx")
    t = lax.axis_index("tp")
    rows = q.shape[0]
    heads = q.shape[1] // HD
    width = out.shape[1]
    subs = width // SUB
    low = lax.rem(t, 2)
    high = t // 2
    sibling = high * 2 + 1 - low
    across = lax.rem(t + n_tp // 2, n_tp)
    has_left = me > 0
    has_right = me < n - 1

    local_in = [
        pltpu.make_async_copy(q_hbm, q, in_sem.at[0]),
        pltpu.make_async_copy(pk_hbm, key_all.at[me], in_sem.at[1]),
        pltpu.make_async_copy(pv_hbm, value_all.at[me], in_sem.at[2]),
        pltpu.make_async_copy(rk_hbm, resp_k.at[1], in_sem.at[3]),
        pltpu.make_async_copy(rv_hbm, resp_v.at[1], in_sem.at[4]),
    ]
    for copy in local_in:
        copy.start()

    barrier = pltpu.get_barrier_semaphore()

    @pl.when(has_left)
    def _():
        pl.semaphore_signal(barrier, inc=1, device_id={"ctx": me - 1}, device_id_type=MESH)

    @pl.when(has_right)
    def _():
        pl.semaphore_signal(barrier, inc=1, device_id={"ctx": me + 1}, device_id_type=MESH)

    for partner in (sibling, across):
        pl.semaphore_signal(barrier, inc=1, device_id={"tp": partner}, device_id_type=MESH)
    peers = 2 + has_left.astype(jnp.int32) + has_right.astype(jnp.int32)
    pl.semaphore_wait(barrier, peers)

    def prompt_copy(which, chunk, src, direction, slot):
        dst = (key_all, value_all)[which].at[chunk]
        return pltpu.make_async_remote_copy(
            src_ref=src,
            dst_ref=dst,
            send_sem=gather_send.at[which, slot],
            recv_sem=gather_recv.at[which, chunk],
            device_id={"ctx": me + direction},
            device_id_type=MESH,
        )

    def response_copy(which):
        return pltpu.make_async_remote_copy(
            src_ref=(rk_hbm, rv_hbm)[which],
            dst_ref=(resp_k, resp_v)[which].at[0],
            send_sem=resp_send.at[which],
            recv_sem=resp_recv.at[which],
            device_id={"ctx": me + 1},
            device_id_type=MESH,
        )

    @pl.when(has_right)
    def _():
        prompt_copy(0, me, pk_hbm, 1, n).start()
        prompt_copy(1, me, pv_hbm, 1, n).start()
        response_copy(0).start()
        response_copy(1).start()

    @pl.when(has_left)
    def _():
        prompt_copy(0, me, pk_hbm, -1, n + 1).start()
        prompt_copy(1, me, pv_hbm, -1, n + 1).start()

    w_copy = pltpu.make_async_copy(w_hbm, w, w_sem)
    w_copy.start()

    base = me * rows
    row_pos = base + lax.broadcasted_iota(jnp.int32, (rows, rows), 0)
    key_pos = base + lax.broadcasted_iota(jnp.int32, (rows, rows), 1)
    first = jnp.zeros((rows, rows), jnp.int32)
    start = jnp.int32(0)
    for r in range(lengths.shape[0]):
        first = jnp.where(row_pos >= start, start, first)
        start = start + lengths[r]
    own = (key_pos >= first) & (key_pos <= row_pos)
    bias[1] = jnp.where(own, 0.0, MASKED)
    bias[0] = jnp.where(key_pos - rows >= first, 0.0, MASKED)

    for copy in local_in:
        copy.wait()

    def extended(values):
        return jnp.concatenate([values, jnp.ones(values.shape, values.dtype)], axis=1)

    def attend(parts, fresh):
        for h in range(heads):
            query = q[:, h * HD : (h + 1) * HD]
            scores = []
            for keys, _, extra in parts:
                s = lax.dot_general(
                    query, keys[...], (((1,), (1,)), ((), ())), preferred_element_type=jnp.float32
                )
                s = s * SCALE
                if extra is not None:
                    s = s + extra[...]
                scores.append(s)
            top = functools.reduce(
                jnp.maximum, [jnp.max(s, axis=1, keepdims=True) for s in scores]
            )
            if not fresh:
                before = tops[h]
                top = jnp.maximum(top, before)
            added = None
            for s, (_, values, _) in zip(scores, parts):
                p = jnp.exp2(s - top).astype(jnp.bfloat16)
                term = jnp.dot(p, extended(values[...]), preferred_element_type=jnp.float32)
                added = term if added is None else added + term
            if fresh:
                acc[h] = added
            else:
                acc[h] = acc[h] * jnp.exp2(before - top) + added
            tops[h] = top

    attend(
        [(key_all.at[me], value_all.at[me], None), (resp_k.at[1], resp_v.at[1], bias.at[1])], True
    )

    @pl.when(has_left)
    def _():
        for which in range(2):
            response_copy(which).wait_recv()

    @pl.when(me == 0)
    def _():
        resp_k[0] = jnp.zeros_like(resp_k[0])
        resp_v[0] = jnp.zeros_like(resp_v[0])

    left_count = me
    right_count = n - 1 - me
    both = jnp.minimum(left_count, right_count)

    def arrival(j):
        s = (j + 1) // 2
        paired = jnp.where(lax.rem(j, 2) == 1, -s, s)
        single = jnp.where(left_count > right_count, both - j, j - both)
        return me + jnp.where(j <= 2 * both, paired, single)

    def take(j):
        chunk = arrival(j)
        for which in range(2):
            ref = (key_all, value_all)[which].at[chunk]
            prompt_copy(which, chunk, ref, 1, chunk).wait_recv()

            @pl.when((chunk < me) & has_right)
            def _():
                prompt_copy(which, chunk, ref, 1, chunk).start()

            @pl.when((chunk > me) & has_left)
            def _():
                prompt_copy(which, chunk, ref, -1, chunk).start()

        return chunk

    chunk = take(jnp.int32(1))
    attend(
        [
            (key_all.at[chunk], value_all.at[chunk], None),
            (resp_k.at[0], resp_v.at[0], bias.at[0]),
        ],
        False,
    )

    def later(j, carry):
        chunk = take(j)
        attend([(key_all.at[chunk], value_all.at[chunk], None)], False)
        return carry

    lax.fori_loop(2, n, later, 0)

    for h in range(heads):
        att[:, h * HD : (h + 1) * HD] = (acc[h, :, :HD] / acc[h, :, HD:]).astype(jnp.bfloat16)

    w_copy.wait()

    def product(block, sub):
        columns = pl.ds(pl.multiple_of(block * width + sub * SUB, SUB), SUB)
        return jnp.dot(att[...], w[:, columns], preferred_element_type=jnp.float32)

    def to_sibling(half, sub):
        return pltpu.make_async_remote_copy(
            src_ref=send1.at[half, sub],
            dst_ref=recv1.at[half, sub],
            send_sem=send1_sem.at[half, sub],
            recv_sem=recv1_sem.at[half, sub],
            device_id={"tp": sibling},
            device_id_type=MESH,
        )

    def to_across(sub):
        return pltpu.make_async_remote_copy(
            src_ref=send2.at[sub],
            dst_ref=recv2.at[sub],
            send_sem=send2_sem.at[sub],
            recv_sem=recv2_sem.at[sub],
            device_id={"tp": across},
            device_id_type=MESH,
        )

    def hand_sibling(half, side, sub):
        send1[half, sub] = product(side * 2 + 1 - low, sub).astype(jnp.bfloat16)
        to_sibling(half, sub).start()

    hand_sibling(0, 1 - high, 0)
    for sub in range(subs):
        if sub + 1 < subs:
            hand_sibling(0, 1 - high, sub + 1)
        mine = product((1 - high) * 2 + low, sub)
        to_sibling(0, sub).wait_recv()
        send2[sub] = (mine + recv1[0, sub].astype(jnp.float32)).astype(jnp.bfloat16)
        to_across(sub).start()
    for sub in range(subs):
        hand_sibling(1, high, sub)
    for sub in range(subs):
        near[sub] = product(high * 2 + low, sub)
    for sub in range(subs):
        to_sibling(1, sub).wait_recv()
        near[sub] = near[sub] + recv1[1, sub].astype(jnp.float32)

    def out_copy(sub):
        columns = pl.ds(sub * SUB, SUB)
        return pltpu.make_async_copy(out.at[:, columns], out_hbm.at[:, columns], out_sem.at[sub])

    for sub in range(subs):
        to_across(sub).wait_recv()
        out[:, sub * SUB : (sub + 1) * SUB] = (
            near[sub] + recv2[sub].astype(jnp.float32)
        ).astype(jnp.bfloat16)
        out_copy(sub).start()

    for sub in range(subs):
        to_sibling(0, sub).wait_send()
        to_sibling(1, sub).wait_send()
        to_across(sub).wait_send()

    @pl.when(has_right)
    def _():
        for which in range(2):
            prompt_copy(which, me, key_all.at[me], 1, n).wait_send()
            response_copy(which).wait_send()

    @pl.when(has_left)
    def _():
        for which in range(2):
            prompt_copy(which, me, key_all.at[me], -1, n + 1).wait_send()

    def drain(j, carry):
        chunk = arrival(j)

        @pl.when(((chunk < me) & has_right) | ((chunk > me) & has_left))
        def _():
            for which in range(2):
                prompt_copy(which, chunk, key_all.at[chunk], 1, chunk).wait_send()

        return carry

    lax.fori_loop(1, n, drain, 0)
    for sub in range(subs):
        out_copy(sub).wait()


def local(mesh_shape, queries, rk, rv, pk, pv, lengths, out_weight):
    n, n_tp = mesh_shape["ctx"], mesh_shape["tp"]
    rows, query_cols = queries.shape
    depth, out_cols = out_weight.shape
    width = out_cols // n_tp
    subs = width // SUB
    heads = query_cols // HD
    assert rk.shape[1] == HD and n_tp == 4
    bf16, f32 = jnp.bfloat16, jnp.float32
    dma = pltpu.SemaphoreType.DMA
    any_space = pl.BlockSpec(memory_space=pl.ANY)
    return pl.pallas_call(
        functools.partial(kernel, n, n_tp),
        out_shape=jax.ShapeDtypeStruct((rows, width), bf16),
        in_specs=[any_space] * 5 + [pl.BlockSpec(memory_space=pltpu.SMEM), any_space],
        out_specs=any_space,
        scratch_shapes=[
            pltpu.VMEM((rows, query_cols), bf16),
            pltpu.VMEM((depth, out_cols), bf16),
            pltpu.VMEM((n, rows, HD), bf16),
            pltpu.VMEM((n, rows, HD), bf16),
            pltpu.VMEM((2, rows, HD), bf16),
            pltpu.VMEM((2, rows, HD), bf16),
            pltpu.VMEM((2, rows, rows), f32),
            pltpu.VMEM((heads, rows, 2 * HD), f32),
            pltpu.VMEM((heads, rows, 1), f32),
            pltpu.VMEM((rows, query_cols), bf16),
            pltpu.VMEM((2, subs, rows, SUB), bf16),
            pltpu.VMEM((2, subs, rows, SUB), bf16),
            pltpu.VMEM((subs, rows, SUB), bf16),
            pltpu.VMEM((subs, rows, SUB), bf16),
            pltpu.VMEM((subs, rows, SUB), f32),
            pltpu.VMEM((rows, width), bf16),
            dma((5,)),
            dma,
            dma((subs,)),
            dma((2, n + 2)),
            dma((2, n)),
            dma((2,)),
            dma((2,)),
            dma((2, subs)),
            dma((2, subs)),
            dma((subs,)),
            dma((subs,)),
        ],
        compiler_params=pltpu.CompilerParams(
            collective_id=0, has_side_effects=True, vmem_limit_bytes=48 * 1024 * 1024
        ),
    )(queries, rk, rv, pk, pv, lengths, out_weight)


def solution(mesh):
    placed = (
        P(("groups", "ctx"), "tp"),
        P(("groups", "ctx"), "tp"),
        P(("groups", "ctx"), "tp"),
        P(("groups", "ctx"), "tp"),
        P(("groups", "ctx"), "tp"),
        P("groups"),
        P("tp", None),
    )
    return jax.shard_map(
        functools.partial(local, dict(mesh.shape)),
        mesh=mesh,
        in_specs=placed,
        out_specs=P(("groups", "ctx"), "tp"),
        check_vma=False,
    )
```

```python
import functools

import jax
import jax.numpy as jnp
from jax import lax
from jax.experimental import pallas as pl
from jax.experimental.pallas import tpu as pltpu
from jax.sharding import PartitionSpec as P

HD = 128
SUB = 256
MESH = pl.DeviceIdType.MESH
SCALE = 1.4426950408889634 / HD**0.5
MASKED = -1e30
VMEM_BYTES = 63 * 1024 * 1024


def kernel(
    n,
    n_tp,
    q_hbm,
    rk_hbm,
    rv_hbm,
    pk_hbm,
    pv_hbm,
    lengths_hbm,
    w_hbm,
    out_hbm,
    lengths,
    q,
    w,
    key_all,
    value_all,
    resp_k,
    resp_v,
    bias,
    acc,
    tops,
    att,
    send1,
    recv1,
    send2,
    recv2,
    near,
    out,
    in_sem,
    w_sem,
    out_sem,
    gather_send,
    gather_recv,
    resp_send,
    resp_recv,
    send1_sem,
    recv1_sem,
    send2_sem,
    recv2_sem,
):
    me = lax.axis_index("ctx")
    t = lax.axis_index("tp")
    rows = q.shape[0]
    heads = q.shape[1] // HD
    width = out.shape[1]
    subs = width // SUB
    low = lax.rem(t, 2)
    high = t // 2
    sibling = high * 2 + 1 - low
    across = lax.rem(t + n_tp // 2, n_tp)
    has_left = me > 0
    has_right = me < n - 1

    local_in = [
        pltpu.make_async_copy(q_hbm, q, in_sem.at[0]),
        pltpu.make_async_copy(pk_hbm, key_all.at[me], in_sem.at[1]),
        pltpu.make_async_copy(pv_hbm, value_all.at[me], in_sem.at[2]),
        pltpu.make_async_copy(rk_hbm, resp_k.at[1], in_sem.at[3]),
        pltpu.make_async_copy(rv_hbm, resp_v.at[1], in_sem.at[4]),
        pltpu.make_async_copy(lengths_hbm, lengths, in_sem.at[5]),
    ]
    for copy in local_in:
        copy.start()

    w_copy = pltpu.make_async_copy(w_hbm, w, w_sem)
    w_copy.start()

    barrier = pltpu.get_barrier_semaphore()

    @pl.when(has_left)
    def _():
        pl.semaphore_signal(barrier, inc=1, device_id={"ctx": me - 1}, device_id_type=MESH)

    @pl.when(has_right)
    def _():
        pl.semaphore_signal(barrier, inc=1, device_id={"ctx": me + 1}, device_id_type=MESH)

    for partner in (sibling, across):
        pl.semaphore_signal(barrier, inc=1, device_id={"tp": partner}, device_id_type=MESH)
    peers = 2 + has_left.astype(jnp.int32) + has_right.astype(jnp.int32)
    pl.semaphore_wait(barrier, peers)

    def prompt_copy(which, chunk, src, direction, slot):
        dst = (key_all, value_all)[which].at[chunk]
        return pltpu.make_async_remote_copy(
            src_ref=src,
            dst_ref=dst,
            send_sem=gather_send.at[which, slot],
            recv_sem=gather_recv.at[which, chunk],
            device_id={"ctx": me + direction},
            device_id_type=MESH,
        )

    def response_copy(which):
        return pltpu.make_async_remote_copy(
            src_ref=(rk_hbm, rv_hbm)[which],
            dst_ref=(resp_k, resp_v)[which].at[0],
            send_sem=resp_send.at[which],
            recv_sem=resp_recv.at[which],
            device_id={"ctx": me + 1},
            device_id_type=MESH,
        )

    @pl.when(has_right)
    def _():
        prompt_copy(0, me, pk_hbm, 1, n).start()
        prompt_copy(1, me, pv_hbm, 1, n).start()

    @pl.when(has_left)
    def _():
        prompt_copy(0, me, pk_hbm, -1, n + 1).start()
        prompt_copy(1, me, pv_hbm, -1, n + 1).start()

    for copy in local_in:
        copy.wait()

    base = me * rows
    row_pos = base + lax.broadcasted_iota(jnp.int32, (rows, rows), 0)
    key_pos = base + lax.broadcasted_iota(jnp.int32, (rows, rows), 1)
    first = jnp.zeros((rows, rows), jnp.int32)
    start = jnp.int32(0)
    for r in range(lengths.shape[0]):
        first = jnp.where(row_pos >= start, start, first)
        start = start + lengths[r]
    own = (key_pos >= first) & (key_pos <= row_pos)
    bias[1] = jnp.where(own, 0.0, MASKED)
    bias[0] = jnp.where(key_pos - rows >= first, 0.0, MASKED)

    def extended(values):
        return jnp.concatenate([values, jnp.ones(values.shape, values.dtype)], axis=1)

    def attend(parts, fresh):
        for h in range(heads):
            query = q[:, h * HD : (h + 1) * HD]
            scores = []
            for keys, _, extra in parts:
                s = lax.dot_general(
                    query, keys[...], (((1,), (1,)), ((), ())), preferred_element_type=jnp.float32
                )
                s = s * SCALE
                if extra is not None:
                    s = s + extra[...]
                scores.append(s)
            top = functools.reduce(
                jnp.maximum, [jnp.max(s, axis=1, keepdims=True) for s in scores]
            )
            if not fresh:
                before = tops[h]
                top = jnp.maximum(top, before)
            added = None
            for s, (_, values, _) in zip(scores, parts):
                p = jnp.exp2(s - top).astype(jnp.bfloat16)
                term = jnp.dot(p, extended(values[...]), preferred_element_type=jnp.float32)
                added = term if added is None else added + term
            if fresh:
                acc[h] = added
            else:
                acc[h] = acc[h] * jnp.exp2(before - top) + added
            tops[h] = top

    attend(
        [(key_all.at[me], value_all.at[me], None), (resp_k.at[1], resp_v.at[1], bias.at[1])], True
    )

    @pl.when(has_right)
    def _():
        response_copy(0).start()
        response_copy(1).start()

    def hand_on(chunk, direction, onward):
        for which in range(2):
            ref = (key_all, value_all)[which].at[chunk]
            copy = prompt_copy(which, chunk, ref, direction, chunk)
            copy.wait_recv()
            pl.when(onward)(copy.start)

    def ring(s, carry):
        from_left, from_right = me - s, me + s

        @pl.when(from_left >= 0)
        def _():
            hand_on(from_left, 1, has_right)

        @pl.when(from_right < n)
        def _():
            hand_on(from_right, -1, has_left)

        @pl.when(from_left >= 0)
        def _():
            attend([(key_all.at[from_left], value_all.at[from_left], None)], False)

        @pl.when(from_right < n)
        def _():
            attend([(key_all.at[from_right], value_all.at[from_right], None)], False)

        @pl.when(has_left & (s == jnp.where(has_right, 2, 1)))
        def _():
            for which in range(2):
                response_copy(which).wait_recv()
            attend([(resp_k.at[0], resp_v.at[0], bias.at[0])], False)

        return carry

    lax.fori_loop(1, n, ring, 0)

    for h in range(heads):
        att[:, h * HD : (h + 1) * HD] = (acc[h, :, :HD] / acc[h, :, HD:]).astype(jnp.bfloat16)

    w_copy.wait()

    def product(block, sub):
        columns = pl.ds(pl.multiple_of(block * width + sub * SUB, SUB), SUB)
        return jnp.dot(att[...], w[:, columns], preferred_element_type=jnp.float32)

    def to_sibling(half, sub):
        return pltpu.make_async_remote_copy(
            src_ref=send1.at[half, sub],
            dst_ref=recv1.at[half, sub],
            send_sem=send1_sem.at[half, sub],
            recv_sem=recv1_sem.at[half, sub],
            device_id={"tp": sibling},
            device_id_type=MESH,
        )

    def to_across(sub):
        return pltpu.make_async_remote_copy(
            src_ref=send2.at[sub],
            dst_ref=recv2.at[sub],
            send_sem=send2_sem.at[sub],
            recv_sem=recv2_sem.at[sub],
            device_id={"tp": across},
            device_id_type=MESH,
        )

    def hand_sibling(half, side, sub):
        send1[half, sub] = product(side * 2 + 1 - low, sub).astype(jnp.bfloat16)
        to_sibling(half, sub).start()

    hand_sibling(0, 1 - high, 0)
    for sub in range(subs):
        if sub + 1 < subs:
            hand_sibling(0, 1 - high, sub + 1)
        mine = product((1 - high) * 2 + low, sub)
        to_sibling(0, sub).wait_recv()
        send2[sub] = (mine + recv1[0, sub].astype(jnp.float32)).astype(jnp.bfloat16)
        to_across(sub).start()
    for sub in range(subs):
        hand_sibling(1, high, sub)
    for sub in range(subs):
        near[sub] = product(high * 2 + low, sub)
    for sub in range(subs):
        to_sibling(1, sub).wait_recv()
        near[sub] = near[sub] + recv1[1, sub].astype(jnp.float32)

    def out_copy(sub):
        columns = pl.ds(sub * SUB, SUB)
        return pltpu.make_async_copy(out.at[:, columns], out_hbm.at[:, columns], out_sem.at[sub])

    for sub in range(subs):
        to_across(sub).wait_recv()
        out[:, sub * SUB : (sub + 1) * SUB] = (
            near[sub] + recv2[sub].astype(jnp.float32)
        ).astype(jnp.bfloat16)
        out_copy(sub).start()

    for sub in range(subs):
        to_sibling(0, sub).wait_send()
        to_sibling(1, sub).wait_send()
        to_across(sub).wait_send()

    @pl.when(has_right)
    def _():
        for which in range(2):
            prompt_copy(which, me, key_all.at[me], 1, n).wait_send()
            response_copy(which).wait_send()

    @pl.when(has_left)
    def _():
        for which in range(2):
            prompt_copy(which, me, key_all.at[me], -1, n + 1).wait_send()

    def drain(chunk, carry):
        @pl.when(((chunk < me) & has_right) | ((chunk > me) & has_left))
        def _():
            for which in range(2):
                prompt_copy(which, chunk, key_all.at[chunk], 1, chunk).wait_send()

        return carry

    lax.fori_loop(0, n, drain, 0)
    for sub in range(subs):
        out_copy(sub).wait()


def local(mesh_shape, queries, rk, rv, pk, pv, lengths, out_weight):
    n, n_tp = mesh_shape["ctx"], mesh_shape["tp"]
    rows, query_cols = queries.shape
    depth, out_cols = out_weight.shape
    width = out_cols // n_tp
    subs = width // SUB
    heads = query_cols // HD
    assert rk.shape[1] == HD and n_tp == 4
    bf16, f32 = jnp.bfloat16, jnp.float32
    dma = pltpu.SemaphoreType.DMA
    in_hbm = pl.BlockSpec(memory_space=pltpu.HBM)
    return pl.pallas_call(
        functools.partial(kernel, n, n_tp),
        out_shape=jax.ShapeDtypeStruct((rows, width), bf16),
        in_specs=[in_hbm] * 7,
        out_specs=in_hbm,
        scratch_shapes=[
            pltpu.SMEM(lengths.shape, jnp.int32),
            pltpu.VMEM((rows, query_cols), bf16),
            pltpu.VMEM((depth, out_cols), bf16),
            pltpu.VMEM((n, rows, HD), bf16),
            pltpu.VMEM((n, rows, HD), bf16),
            pltpu.VMEM((2, rows, HD), bf16),
            pltpu.VMEM((2, rows, HD), bf16),
            pltpu.VMEM((2, rows, rows), f32),
            pltpu.VMEM((heads, rows, 2 * HD), f32),
            pltpu.VMEM((heads, rows, 1), f32),
            pltpu.VMEM((rows, query_cols), bf16),
            pltpu.VMEM((2, subs, rows, SUB), bf16),
            pltpu.VMEM((2, subs, rows, SUB), bf16),
            pltpu.VMEM((subs, rows, SUB), bf16),
            pltpu.VMEM((subs, rows, SUB), bf16),
            pltpu.VMEM((subs, rows, SUB), f32),
            pltpu.VMEM((rows, width), bf16),
            dma((6,)),
            dma,
            dma((subs,)),
            dma((2, n + 2)),
            dma((2, n)),
            dma((2,)),
            dma((2,)),
            dma((2, subs)),
            dma((2, subs)),
            dma((subs,)),
            dma((subs,)),
        ],
        compiler_params=pltpu.CompilerParams(
            collective_id=0, has_side_effects=True, vmem_limit_bytes=VMEM_BYTES
        ),
    )(queries, rk, rv, pk, pv, lengths, out_weight)


def solution(mesh):
    placed = (
        P(("groups", "ctx"), "tp"),
        P(("groups", "ctx"), "tp"),
        P(("groups", "ctx"), "tp"),
        P(("groups", "ctx"), "tp"),
        P(("groups", "ctx"), "tp"),
        P("groups"),
        P("tp", None),
    )
    return jax.shard_map(
        functools.partial(local, dict(mesh.shape)),
        mesh=mesh,
        in_specs=placed,
        out_specs=P(("groups", "ctx"), "tp"),
        check_vma=False,
    )
```

```python
import functools

import jax
import jax.numpy as jnp
from jax import lax
from jax.experimental import pallas as pl
from jax.experimental.pallas import tpu as pltpu
from jax.sharding import PartitionSpec as P

HD = 128
SUB = 256
MESH = pl.DeviceIdType.MESH
SCALE = 1.4426950408889634 / HD**0.5
MASKED = -1e30
VMEM_BYTES = 62 * 1024 * 1024


def kernel(
    n,
    n_tp,
    q_hbm,
    rk_hbm,
    rv_hbm,
    pk_hbm,
    pv_hbm,
    lengths_hbm,
    w_hbm,
    out,
    lengths,
    q,
    w,
    key_all,
    value_all,
    resp_k,
    resp_v,
    bias,
    acc,
    tops,
    att,
    send1,
    recv1,
    send2,
    recv2,
    near,
    in_sem,
    w_sem,
    gather_send,
    gather_recv,
    resp_send,
    resp_recv,
    send1_sem,
    recv1_sem,
    send2_sem,
    recv2_sem,
):
    me = lax.axis_index("ctx")
    t = lax.axis_index("tp")
    rows = q.shape[0]
    heads = q.shape[1] // HD
    width = out.shape[1]
    subs = width // SUB
    low = lax.rem(t, 2)
    high = t // 2
    sibling = high * 2 + 1 - low
    across = lax.rem(t + n_tp // 2, n_tp)
    has_left = me > 0
    has_right = me < n - 1

    local_in = [
        pltpu.make_async_copy(q_hbm, q, in_sem.at[0]),
        pltpu.make_async_copy(pk_hbm, key_all.at[me], in_sem.at[1]),
        pltpu.make_async_copy(pv_hbm, value_all.at[me], in_sem.at[2]),
        pltpu.make_async_copy(rk_hbm, resp_k.at[1], in_sem.at[3]),
        pltpu.make_async_copy(rv_hbm, resp_v.at[1], in_sem.at[4]),
        pltpu.make_async_copy(lengths_hbm, lengths, in_sem.at[5]),
    ]
    for copy in local_in:
        copy.start()

    w_copy = pltpu.make_async_copy(w_hbm, w, w_sem)
    w_copy.start()

    barrier = pltpu.get_barrier_semaphore()

    @pl.when(has_left)
    def _():
        pl.semaphore_signal(barrier, inc=1, device_id={"ctx": me - 1}, device_id_type=MESH)

    @pl.when(has_right)
    def _():
        pl.semaphore_signal(barrier, inc=1, device_id={"ctx": me + 1}, device_id_type=MESH)

    for partner in (sibling, across):
        pl.semaphore_signal(barrier, inc=1, device_id={"tp": partner}, device_id_type=MESH)
    peers = 2 + has_left.astype(jnp.int32) + has_right.astype(jnp.int32)
    for copy in local_in:
        copy.wait()

    base = me * rows
    row_pos = base + lax.broadcasted_iota(jnp.int32, (rows, rows), 0)
    key_pos = base + lax.broadcasted_iota(jnp.int32, (rows, rows), 1)
    first = jnp.zeros((rows, rows), jnp.int32)
    start = jnp.int32(0)
    for r in range(lengths.shape[0]):
        first = jnp.where(row_pos >= start, start, first)
        start = start + lengths[r]
    own = (key_pos >= first) & (key_pos <= row_pos)
    bias[1] = jnp.where(own, 0.0, MASKED)
    bias[0] = jnp.where(key_pos - rows >= first, 0.0, MASKED)

    pl.semaphore_wait(barrier, peers)

    def prompt_copy(which, chunk, src, direction, slot):
        dst = (key_all, value_all)[which].at[chunk]
        return pltpu.make_async_remote_copy(
            src_ref=src,
            dst_ref=dst,
            send_sem=gather_send.at[which, slot],
            recv_sem=gather_recv.at[which, chunk],
            device_id={"ctx": me + direction},
            device_id_type=MESH,
        )

    def response_copy(which):
        return pltpu.make_async_remote_copy(
            src_ref=(rk_hbm, rv_hbm)[which],
            dst_ref=(resp_k, resp_v)[which].at[0],
            send_sem=resp_send.at[which],
            recv_sem=resp_recv.at[which],
            device_id={"ctx": me + 1},
            device_id_type=MESH,
        )

    @pl.when(has_right)
    def _():
        prompt_copy(0, me, pk_hbm, 1, n).start()
        prompt_copy(1, me, pv_hbm, 1, n).start()

    @pl.when(has_left)
    def _():
        prompt_copy(0, me, pk_hbm, -1, n + 1).start()
        prompt_copy(1, me, pv_hbm, -1, n + 1).start()

    def extended(values):
        return jnp.concatenate([values, jnp.ones(values.shape, values.dtype)], axis=1)

    def attend(parts, fresh):
        for h in range(heads):
            query = q[:, h * HD : (h + 1) * HD]
            scores = []
            for keys, _, extra in parts:
                s = lax.dot_general(
                    query, keys[...], (((1,), (1,)), ((), ())), preferred_element_type=jnp.float32
                )
                s = s * SCALE
                if extra is not None:
                    s = s + extra[...]
                scores.append(s)
            top = functools.reduce(
                jnp.maximum, [jnp.max(s, axis=1, keepdims=True) for s in scores]
            )
            if not fresh:
                before = tops[h]
                top = jnp.maximum(top, before)
            added = None
            for s, (_, values, _) in zip(scores, parts):
                p = jnp.exp2(s - top).astype(jnp.bfloat16)
                term = jnp.dot(p, extended(values[...]), preferred_element_type=jnp.float32)
                added = term if added is None else added + term
            if fresh:
                acc[h] = added
            else:
                acc[h] = acc[h] * jnp.exp2(before - top) + added
            tops[h] = top

    attend(
        [(key_all.at[me], value_all.at[me], None), (resp_k.at[1], resp_v.at[1], bias.at[1])], True
    )

    @pl.when(has_right)
    def _():
        response_copy(0).start()
        response_copy(1).start()

    def hand_on(chunk, direction, onward):
        for which in range(2):
            ref = (key_all, value_all)[which].at[chunk]
            copy = prompt_copy(which, chunk, ref, direction, chunk)
            copy.wait_recv()
            pl.when(onward)(copy.start)

    def ring(s, carry):
        from_left, from_right = me - s, me + s

        @pl.when(from_left >= 0)
        def _():
            hand_on(from_left, 1, has_right)

        @pl.when(from_right < n)
        def _():
            hand_on(from_right, -1, has_left)

        @pl.when(from_left >= 0)
        def _():
            attend([(key_all.at[from_left], value_all.at[from_left], None)], False)

        @pl.when(from_right < n)
        def _():
            attend([(key_all.at[from_right], value_all.at[from_right], None)], False)

        @pl.when(has_left & (s == jnp.where(has_right, 2, 1)))
        def _():
            for which in range(2):
                response_copy(which).wait_recv()
            attend([(resp_k.at[0], resp_v.at[0], bias.at[0])], False)

        return carry

    lax.fori_loop(1, n, ring, 0)

    for h in range(heads):
        att[:, h * HD : (h + 1) * HD] = (acc[h, :, :HD] / acc[h, :, HD:]).astype(jnp.bfloat16)

    w_copy.wait()

    def product(block, sub):
        columns = pl.ds(pl.multiple_of(block * width + sub * SUB, SUB), SUB)
        return jnp.dot(att[...], w[:, columns], preferred_element_type=jnp.float32)

    def to_sibling(half, sub):
        return pltpu.make_async_remote_copy(
            src_ref=send1.at[half, sub],
            dst_ref=recv1.at[half, sub],
            send_sem=send1_sem.at[half, sub],
            recv_sem=recv1_sem.at[half, sub],
            device_id={"tp": sibling},
            device_id_type=MESH,
        )

    def to_across(sub):
        return pltpu.make_async_remote_copy(
            src_ref=send2.at[sub],
            dst_ref=recv2.at[sub],
            send_sem=send2_sem.at[sub],
            recv_sem=recv2_sem.at[sub],
            device_id={"tp": across},
            device_id_type=MESH,
        )

    def hand_sibling(half, side, sub):
        send1[half, sub] = product(side * 2 + 1 - low, sub).astype(jnp.bfloat16)
        to_sibling(half, sub).start()

    hand_sibling(0, 1 - high, 0)
    for sub in range(subs):
        if sub + 1 < subs:
            hand_sibling(0, 1 - high, sub + 1)
        mine = product((1 - high) * 2 + low, sub)
        to_sibling(0, sub).wait_recv()
        send2[sub] = (mine + recv1[0, sub].astype(jnp.float32)).astype(jnp.bfloat16)
        to_across(sub).start()
    for sub in range(subs):
        hand_sibling(1, high, sub)
    for sub in range(subs):
        near[sub] = product(high * 2 + low, sub)
    for sub in range(subs):
        to_sibling(1, sub).wait_recv()
        near[sub] = near[sub] + recv1[1, sub].astype(jnp.float32)

    for sub in range(subs):
        to_across(sub).wait_recv()
        out[:, sub * SUB : (sub + 1) * SUB] = (
            near[sub] + recv2[sub].astype(jnp.float32)
        ).astype(jnp.bfloat16)

    for sub in range(subs):
        to_sibling(0, sub).wait_send()
        to_sibling(1, sub).wait_send()
        to_across(sub).wait_send()

    @pl.when(has_right)
    def _():
        for which in range(2):
            prompt_copy(which, me, key_all.at[me], 1, n).wait_send()
            response_copy(which).wait_send()

    @pl.when(has_left)
    def _():
        for which in range(2):
            prompt_copy(which, me, key_all.at[me], -1, n + 1).wait_send()

    def drain(chunk, carry):
        @pl.when(((chunk < me) & has_right) | ((chunk > me) & has_left))
        def _():
            for which in range(2):
                prompt_copy(which, chunk, key_all.at[chunk], 1, chunk).wait_send()

        return carry

    lax.fori_loop(0, n, drain, 0)


def local(mesh_shape, queries, rk, rv, pk, pv, lengths, out_weight):
    n, n_tp = mesh_shape["ctx"], mesh_shape["tp"]
    rows, query_cols = queries.shape
    depth, out_cols = out_weight.shape
    width = out_cols // n_tp
    subs = width // SUB
    heads = query_cols // HD
    assert rk.shape[1] == HD and n_tp == 4
    bf16, f32 = jnp.bfloat16, jnp.float32
    dma = pltpu.SemaphoreType.DMA
    in_hbm = pl.BlockSpec(memory_space=pltpu.HBM)
    return pl.pallas_call(
        functools.partial(kernel, n, n_tp),
        out_shape=pltpu.VMEM((rows, width), bf16),
        in_specs=[in_hbm] * 7,
        out_specs=pl.BlockSpec(memory_space=pltpu.VMEM),
        scratch_shapes=[
            pltpu.SMEM(lengths.shape, jnp.int32),
            pltpu.VMEM((rows, query_cols), bf16),
            pltpu.VMEM((depth, out_cols), bf16),
            pltpu.VMEM((n, rows, HD), bf16),
            pltpu.VMEM((n, rows, HD), bf16),
            pltpu.VMEM((2, rows, HD), bf16),
            pltpu.VMEM((2, rows, HD), bf16),
            pltpu.VMEM((2, rows, rows), f32),
            pltpu.VMEM((heads, rows, 2 * HD), f32),
            pltpu.VMEM((heads, rows, 1), f32),
            pltpu.VMEM((rows, query_cols), bf16),
            pltpu.VMEM((2, subs, rows, SUB), bf16),
            pltpu.VMEM((2, subs, rows, SUB), bf16),
            pltpu.VMEM((subs, rows, SUB), bf16),
            pltpu.VMEM((subs, rows, SUB), bf16),
            pltpu.VMEM((subs, rows, SUB), f32),
            dma((6,)),
            dma,
            dma((2, n + 2)),
            dma((2, n)),
            dma((2,)),
            dma((2,)),
            dma((2, subs)),
            dma((2, subs)),
            dma((subs,)),
            dma((subs,)),
        ],
        compiler_params=pltpu.CompilerParams(
            collective_id=0, has_side_effects=True, vmem_limit_bytes=VMEM_BYTES
        ),
    )(queries, rk, rv, pk, pv, lengths, out_weight)


def solution(mesh):
    placed = (
        P(("groups", "ctx"), "tp"),
        P(("groups", "ctx"), "tp"),
        P(("groups", "ctx"), "tp"),
        P(("groups", "ctx"), "tp"),
        P(("groups", "ctx"), "tp"),
        P("groups"),
        P("tp", None),
    )
    return jax.shard_map(
        functools.partial(local, dict(mesh.shape)),
        mesh=mesh,
        in_specs=placed,
        out_specs=P(("groups", "ctx"), "tp"),
        check_vma=False,
    )
```

```python
import functools

import jax
import jax.numpy as jnp
from jax import lax
from jax.experimental import pallas as pl
from jax.experimental.pallas import tpu as pltpu
from jax.sharding import PartitionSpec as P

HD = 128
SUB = 256
MESH = pl.DeviceIdType.MESH
SCALE = 1.4426950408889634 / HD**0.5
MASKED = -1e30
VMEM_BYTES = 62 * 1024 * 1024


def kernel(
    n,
    n_tp,
    q_hbm,
    rk_hbm,
    rv_hbm,
    pk_hbm,
    pv_hbm,
    lengths_hbm,
    w_hbm,
    out,
    lengths,
    q,
    w,
    key_all,
    value_all,
    resp_k,
    resp_v,
    bias,
    acc,
    tops,
    att,
    send1,
    recv1,
    send2,
    recv2,
    near,
    in_sem,
    w_sem,
    gather_send,
    gather_recv,
    resp_send,
    resp_recv,
    send1_sem,
    recv1_sem,
    send2_sem,
    recv2_sem,
):
    me = lax.axis_index("ctx")
    t = lax.axis_index("tp")
    rows = q.shape[0]
    heads = q.shape[1] // HD
    width = out.shape[1]
    subs = width // SUB
    low = lax.rem(t, 2)
    high = t // 2
    sibling = high * 2 + 1 - low
    across = lax.rem(t + n_tp // 2, n_tp)
    has_left = me > 0
    has_right = me < n - 1

    local_in = [
        pltpu.make_async_copy(q_hbm, q, in_sem.at[0]),
        pltpu.make_async_copy(pk_hbm, key_all.at[me], in_sem.at[1]),
        pltpu.make_async_copy(pv_hbm, value_all.at[me], in_sem.at[2]),
        pltpu.make_async_copy(rk_hbm, resp_k.at[1], in_sem.at[3]),
        pltpu.make_async_copy(rv_hbm, resp_v.at[1], in_sem.at[4]),
        pltpu.make_async_copy(lengths_hbm, lengths, in_sem.at[5]),
    ]
    for copy in local_in:
        copy.start()

    w_copy = pltpu.make_async_copy(w_hbm, w, w_sem)
    w_copy.start()

    barrier = pltpu.get_barrier_semaphore()

    @pl.when(has_left)
    def _():
        pl.semaphore_signal(barrier, inc=1, device_id={"ctx": me - 1}, device_id_type=MESH)

    @pl.when(has_right)
    def _():
        pl.semaphore_signal(barrier, inc=1, device_id={"ctx": me + 1}, device_id_type=MESH)

    for partner in (sibling, across):
        pl.semaphore_signal(barrier, inc=1, device_id={"tp": partner}, device_id_type=MESH)
    peers = 2 + has_left.astype(jnp.int32) + has_right.astype(jnp.int32)
    for copy in local_in:
        copy.wait()

    base = me * rows
    row_pos = base + lax.broadcasted_iota(jnp.int32, (rows, rows), 0)
    key_pos = base + lax.broadcasted_iota(jnp.int32, (rows, rows), 1)
    first = jnp.zeros((rows, rows), jnp.int32)
    start = jnp.int32(0)
    for r in range(lengths.shape[0]):
        first = jnp.where(row_pos >= start, start, first)
        start = start + lengths[r]
    own = (key_pos >= first) & (key_pos <= row_pos)
    bias[1] = jnp.where(own, 0.0, MASKED)
    bias[0] = jnp.where(key_pos - rows >= first, 0.0, MASKED)

    pl.semaphore_wait(barrier, peers)

    def prompt_copy(which, chunk, src, direction, slot):
        dst = (key_all, value_all)[which].at[chunk]
        return pltpu.make_async_remote_copy(
            src_ref=src,
            dst_ref=dst,
            send_sem=gather_send.at[which, slot],
            recv_sem=gather_recv.at[which, chunk],
            device_id={"ctx": me + direction},
            device_id_type=MESH,
        )

    def response_copy(which):
        return pltpu.make_async_remote_copy(
            src_ref=(rk_hbm, rv_hbm)[which],
            dst_ref=(resp_k, resp_v)[which].at[0],
            send_sem=resp_send.at[which],
            recv_sem=resp_recv.at[which],
            device_id={"ctx": me + 1},
            device_id_type=MESH,
        )

    @pl.when(has_right)
    def _():
        prompt_copy(0, me, pk_hbm, 1, n).start()
        prompt_copy(1, me, pv_hbm, 1, n).start()

    @pl.when(has_left)
    def _():
        prompt_copy(0, me, pk_hbm, -1, n + 1).start()
        prompt_copy(1, me, pv_hbm, -1, n + 1).start()

    def extended(values):
        return jnp.concatenate([values, jnp.ones(values.shape, values.dtype)], axis=1)

    def attend(parts, fresh):
        for h in range(heads):
            query = q[:, h * HD : (h + 1) * HD]
            scores = []
            for keys, _, extra in parts:
                s = lax.dot_general(
                    query, keys[...], (((1,), (1,)), ((), ())), preferred_element_type=jnp.float32
                )
                if extra is not None:
                    s = s + extra[...]
                scores.append(s)
            top = functools.reduce(
                jnp.maximum, [jnp.max(s, axis=1, keepdims=True) for s in scores]
            )
            if not fresh:
                before = tops[h]
                top = jnp.maximum(top, before)
            added = None
            for s, (_, values, _) in zip(scores, parts):
                p = jnp.exp2((s - top) * SCALE).astype(jnp.bfloat16)
                term = jnp.dot(p, extended(values[...]), preferred_element_type=jnp.float32)
                added = term if added is None else added + term
            if fresh:
                acc[h] = added
            else:
                acc[h] = acc[h] * jnp.exp2((before - top) * SCALE) + added
            tops[h] = top

    attend(
        [(key_all.at[me], value_all.at[me], None), (resp_k.at[1], resp_v.at[1], bias.at[1])], True
    )

    @pl.when(has_right)
    def _():
        response_copy(0).start()
        response_copy(1).start()

    def hand_on(chunk, direction, onward):
        for which in range(2):
            ref = (key_all, value_all)[which].at[chunk]
            copy = prompt_copy(which, chunk, ref, direction, chunk)
            copy.wait_recv()
            pl.when(onward)(copy.start)

    def ring(s, carry):
        from_left, from_right = me - s, me + s

        @pl.when(from_left >= 0)
        def _():
            hand_on(from_left, 1, has_right)

        @pl.when(from_right < n)
        def _():
            hand_on(from_right, -1, has_left)

        @pl.when(from_left >= 0)
        def _():
            attend([(key_all.at[from_left], value_all.at[from_left], None)], False)

        @pl.when(from_right < n)
        def _():
            attend([(key_all.at[from_right], value_all.at[from_right], None)], False)

        @pl.when(has_left & (s == jnp.where(has_right, 2, 1)))
        def _():
            for which in range(2):
                response_copy(which).wait_recv()
            attend([(resp_k.at[0], resp_v.at[0], bias.at[0])], False)

        return carry

    lax.fori_loop(1, n, ring, 0)

    for h in range(heads):
        att[:, h * HD : (h + 1) * HD] = (acc[h, :, :HD] / acc[h, :, HD:]).astype(jnp.bfloat16)

    w_copy.wait()

    def product(block, sub):
        columns = pl.ds(pl.multiple_of(block * width + sub * SUB, SUB), SUB)
        return jnp.dot(att[...], w[:, columns], preferred_element_type=jnp.float32)

    def to_sibling(half, sub):
        return pltpu.make_async_remote_copy(
            src_ref=send1.at[half, sub],
            dst_ref=recv1.at[half, sub],
            send_sem=send1_sem.at[half, sub],
            recv_sem=recv1_sem.at[half, sub],
            device_id={"tp": sibling},
            device_id_type=MESH,
        )

    def to_across(sub):
        return pltpu.make_async_remote_copy(
            src_ref=send2.at[sub],
            dst_ref=recv2.at[sub],
            send_sem=send2_sem.at[sub],
            recv_sem=recv2_sem.at[sub],
            device_id={"tp": across},
            device_id_type=MESH,
        )

    def hand_sibling(half, side, sub):
        send1[half, sub] = product(side * 2 + 1 - low, sub).astype(jnp.bfloat16)
        to_sibling(half, sub).start()

    hand_sibling(0, 1 - high, 0)
    for sub in range(subs):
        if sub + 1 < subs:
            hand_sibling(0, 1 - high, sub + 1)
        mine = product((1 - high) * 2 + low, sub)
        to_sibling(0, sub).wait_recv()
        send2[sub] = (mine + recv1[0, sub].astype(jnp.float32)).astype(jnp.bfloat16)
        to_across(sub).start()
    for sub in range(subs):
        hand_sibling(1, high, sub)
    for sub in range(subs):
        near[sub] = product(high * 2 + low, sub)
    for sub in range(subs):
        to_sibling(1, sub).wait_recv()
        near[sub] = near[sub] + recv1[1, sub].astype(jnp.float32)

    for sub in range(subs):
        to_across(sub).wait_recv()
        out[:, sub * SUB : (sub + 1) * SUB] = (
            near[sub] + recv2[sub].astype(jnp.float32)
        ).astype(jnp.bfloat16)

    for sub in range(subs):
        to_sibling(0, sub).wait_send()
        to_sibling(1, sub).wait_send()
        to_across(sub).wait_send()

    @pl.when(has_right)
    def _():
        for which in range(2):
            prompt_copy(which, me, key_all.at[me], 1, n).wait_send()
            response_copy(which).wait_send()

    @pl.when(has_left)
    def _():
        for which in range(2):
            prompt_copy(which, me, key_all.at[me], -1, n + 1).wait_send()

    def drain(chunk, carry):
        @pl.when(((chunk < me) & has_right) | ((chunk > me) & has_left))
        def _():
            for which in range(2):
                prompt_copy(which, chunk, key_all.at[chunk], 1, chunk).wait_send()

        return carry

    lax.fori_loop(0, n, drain, 0)


def local(mesh_shape, queries, rk, rv, pk, pv, lengths, out_weight):
    n, n_tp = mesh_shape["ctx"], mesh_shape["tp"]
    rows, query_cols = queries.shape
    depth, out_cols = out_weight.shape
    width = out_cols // n_tp
    subs = width // SUB
    heads = query_cols // HD
    assert rk.shape[1] == HD and n_tp == 4
    bf16, f32 = jnp.bfloat16, jnp.float32
    dma = pltpu.SemaphoreType.DMA
    in_hbm = pl.BlockSpec(memory_space=pltpu.HBM)
    return pl.pallas_call(
        functools.partial(kernel, n, n_tp),
        out_shape=pltpu.VMEM((rows, width), bf16),
        in_specs=[in_hbm] * 7,
        out_specs=pl.BlockSpec(memory_space=pltpu.VMEM),
        scratch_shapes=[
            pltpu.SMEM(lengths.shape, jnp.int32),
            pltpu.VMEM((rows, query_cols), bf16),
            pltpu.VMEM((depth, out_cols), bf16),
            pltpu.VMEM((n, rows, HD), bf16),
            pltpu.VMEM((n, rows, HD), bf16),
            pltpu.VMEM((2, rows, HD), bf16),
            pltpu.VMEM((2, rows, HD), bf16),
            pltpu.VMEM((2, rows, rows), f32),
            pltpu.VMEM((heads, rows, 2 * HD), f32),
            pltpu.VMEM((heads, rows, 1), f32),
            pltpu.VMEM((rows, query_cols), bf16),
            pltpu.VMEM((2, subs, rows, SUB), bf16),
            pltpu.VMEM((2, subs, rows, SUB), bf16),
            pltpu.VMEM((subs, rows, SUB), bf16),
            pltpu.VMEM((subs, rows, SUB), bf16),
            pltpu.VMEM((subs, rows, SUB), f32),
            dma((6,)),
            dma,
            dma((2, n + 2)),
            dma((2, n)),
            dma((2,)),
            dma((2,)),
            dma((2, subs)),
            dma((2, subs)),
            dma((subs,)),
            dma((subs,)),
        ],
        compiler_params=pltpu.CompilerParams(
            collective_id=0, has_side_effects=True, vmem_limit_bytes=VMEM_BYTES
        ),
    )(queries, rk, rv, pk, pv, lengths, out_weight)


def solution(mesh):
    placed = (
        P(("groups", "ctx"), "tp"),
        P(("groups", "ctx"), "tp"),
        P(("groups", "ctx"), "tp"),
        P(("groups", "ctx"), "tp"),
        P(("groups", "ctx"), "tp"),
        P("groups"),
        P("tp", None),
    )
    return jax.shard_map(
        functools.partial(local, dict(mesh.shape)),
        mesh=mesh,
        in_specs=placed,
        out_specs=P(("groups", "ctx"), "tp"),
        check_vma=False,
    )
```
